256 devices in a mesh: dp: 64 (over y, z, core), head: 4 (over x).
Axes of the slice: x: 4, y: 4, z: 8, core: 2. Of those that a mesh axis runs over, the one named last changes fastest.
Arguments:
- queries: bfloat16 [256, 2, 128, 576], P('dp', None, 'head'), may hold values from -200 to 200
- new_entries: bfloat16 [256, 2, 576], P('dp'), may hold values from -4 to 4
- cache: bfloat16 [256, 1024, 576], P('dp'), may hold values from -3 to 3
- lengths: int32 [256], P('dp'), may hold values from 64 to 1024, as said below
- hidden: bfloat16 [256, 2, 7168], P(None, None, 'dp'), may hold values from -1.1953125 to 1.1953125
- w_uv: bfloat16 [128, 512, 128], P('head'), may hold values from -0.25 to 0.25
- w_o: bfloat16 [16384, 7168], P('head', 'dp'), may hold values from -0.09375 to 0.09375
- ffn_gain: bfloat16 [7168], replicated, may hold values from 0.099609375 to 1.8984375
- w_gate: bfloat16 [7168, 18432], P('head', 'dp'), may hold values from -0.0625 to 0.0625
- w_up: bfloat16 [7168, 18432], P('head', 'dp'), may hold values from -0.0625 to 0.0625
- w_down: bfloat16 [18432, 7168], P('dp', 'head'), may hold values from -0.09375 to 0.09375
Outputs:
- layer_out: bfloat16 [256, 2, 7168], P('dp', None, 'head')
The draws below stay inside these ranges and needn't reach their ends.
Inputs may be any that keep to these rules, and one draw needn't show every extreme that they name: Each rollout's cache holds lengths[b] used positions; some rollout has 1024 and some has 64.
All inputs are finite; a program needn't handle non-finite values.
Results may differ from the reference program's by a relative error of at most 0.024.
Values may be sent and summed in bfloat16 or wider, within the bound.
No kernel may reach another device: no remote copies, remote signals or barrier semaphores. Data moves between devices by JAX's collectives and lax.ppermute only.
A program may use at most 128 MiB of HBM per device.

```python
import jax
import jax.numpy as jnp
from jax import lax

D = 7168
H = 128
KV = 512
ROPE = 64
NOPE = 128
VD = 128
FF = 18432
LMAX = 1024
LMIN = 64
ENTRY = 576
B = 256


def shared_cache(key):
    return jax.random.truncated_normal(key, -3.0, 3.0, (B, LMAX, ENTRY), jnp.float32)


def draw_cache(key, part):
    base = shared_cache(key)
    return base.astype(jnp.bfloat16)


def draw_queries(key, part):
    key = jax.random.fold_in(key, 7)
    values = jax.random.truncated_normal(key, -4.0, 4.0, (B, 2, H, ENTRY), jnp.float32)
    return values.astype(jnp.bfloat16)


def draw_lengths(key, part):
    key = jax.random.fold_in(key, 5)
    shift_key, extra_key = jax.random.split(key)
    shifts = jax.random.randint(shift_key, (B,), 0, 5)
    floor_len = jnp.right_shift(jnp.int32(LMAX), shifts)
    extra = jax.random.randint(extra_key, (B,), 0, jnp.right_shift(floor_len, 1) + 1)
    lengths = jnp.clip(floor_len + extra, LMIN, LMAX).astype(jnp.int32)
    lengths = lengths.at[0].set(LMAX)
    lengths = lengths.at[B - 1].set(LMIN)
    return lengths


def steps_of(rng, dims, pieces, low, high):
    factor_of = 1.0
    for dim, parts in pieces:
        steps = jax.random.uniform(jax.random.fold_in(jax.random.fold_in(rng, 6), dim), (parts,), jnp.float32, low / len(pieces), high / len(pieces))
        factor_of = factor_of * jnp.repeat(jnp.exp(steps), dims[dim] // parts).reshape((-1,) + (1,) * (len(dims) - 1 - dim))
    return factor_of


def bell_draw(key, extent, deviation, most, cuts=(), kind=jnp.bfloat16):
    result = jax.random.normal(key, extent, jnp.float32) * deviation
    if len(cuts) > 0:
        result = steps_of(key, extent, cuts, -0.22, 0.18) * result
    return jnp.clip(result, min=-most, max=most).astype(kind)


def setup_inputs(seed: int = 0) -> dict:
    keys = jax.random.split(jax.random.key(seed), 12)
    return {
        "queries": draw_queries(jax.random.fold_in(keys[11], 71), 0),
        "new_entries": bell_draw(keys[1], (B, 2, ENTRY), 1.0, 4.0, ((0, 64),)),
        "cache": draw_cache(jax.random.fold_in(keys[11], 71), 0),
        "lengths": draw_lengths(jax.random.fold_in(keys[11], 71), 0),
        "hidden": bell_draw(keys[4], (B, 2, D), 0.2, 1.1953125, ((2, 64),)),
        "w_uv": bell_draw(keys[5], (H, KV, VD), KV ** -0.5, 0.25, ((0, 4),)),
        "w_o": bell_draw(keys[6], (H * VD, D), (H * VD // 4) ** -0.5, 0.09375, ((0, 4), (1, 64))),
        "ffn_gain": jnp.clip(1.0 + 0.18 * jax.random.normal(keys[7], (D,), jnp.float32), 0.099609375, 1.8984375).astype(jnp.bfloat16),
        "w_gate": bell_draw(keys[8], (D, FF), D ** -0.5, 0.0625, ((0, 4), (1, 64))),
        "w_up": bell_draw(keys[9], (D, FF), D ** -0.5, 0.0625, ((0, 4), (1, 64))),
        "w_down": bell_draw(keys[10], (FF, D), (FF // 4) ** -0.5, 0.09375, ((0, 64), (1, 4))),
    }


def attend_one(args):
    query, new, cache, length = args
    scale = (NOPE + ROPE) ** (-0.5)
    rows = query.reshape(2 * H, ENTRY)
    cache_scores = jnp.dot(rows, cache.T, preferred_element_type=jnp.float32) * scale
    new_scores = jnp.dot(rows, new.T, preferred_element_type=jnp.float32) * scale
    valid = jnp.arange(LMAX, dtype=jnp.int32) < length
    cache_scores = jnp.where(valid[None, :], cache_scores, -1e+30)
    step_of_row = jnp.arange(2 * H, dtype=jnp.int32) // H
    causal = jnp.arange(2, dtype=jnp.int32)[None, :] <= step_of_row[:, None]
    new_scores = jnp.where(causal, new_scores, -1e+30)
    top = jnp.maximum(lax.optimization_barrier(jnp.max(cache_scores, axis=1)), lax.optimization_barrier(jnp.max(new_scores, axis=1)))
    cache_exp = jnp.exp(cache_scores - top[:, None])
    new_exp = jnp.exp(new_scores - top[:, None])
    total = lax.optimization_barrier(jnp.sum(cache_exp, axis=1)) + lax.optimization_barrier(jnp.sum(new_exp, axis=1))
    cache_weights = (cache_exp / total[:, None]).astype(jnp.bfloat16)
    new_weights = (new_exp / total[:, None]).astype(jnp.bfloat16)
    latent = jnp.dot(cache_weights, cache[:, :KV], preferred_element_type=jnp.float32)
    latent = latent + jnp.dot(new_weights, new[:, :KV], preferred_element_type=jnp.float32)
    return latent.astype(jnp.bfloat16).reshape(2, H, KV)

def reference(queries, new_entries, cache, lengths, hidden, w_uv, w_o, ffn_gain, w_gate, w_up, w_down):
    latent_out = lax.map(attend_one, (queries, new_entries, cache, lengths))
    head_out = jnp.einsum('bthc,hcv->bthv', latent_out.astype(jnp.float32), w_uv.astype(jnp.float32))
    head_out = head_out.astype(jnp.bfloat16).reshape(B * 2, H * VD)
    attn = jnp.dot(head_out, w_o, preferred_element_type=jnp.float32)
    resid = (hidden.reshape(B * 2, D).astype(jnp.float32) + attn).astype(jnp.bfloat16)
    resid_f = resid.astype(jnp.float32)
    mean_sq = lax.optimization_barrier(jnp.mean(resid_f * resid_f, axis=1, keepdims=True))
    normed = (resid_f * lax.rsqrt(mean_sq + 1e-06) * ffn_gain.astype(jnp.float32)[None, :]).astype(jnp.bfloat16)
    gate = jnp.dot(normed, w_gate, preferred_element_type=jnp.float32)
    up = jnp.dot(normed, w_up, preferred_element_type=jnp.float32)
    act = (jax.nn.silu(gate) * up).astype(jnp.bfloat16)
    ffn = jnp.dot(act, w_down, preferred_element_type=jnp.float32)
    return (resid_f + ffn).astype(jnp.bfloat16).reshape(B, 2, D)
```

```python
import jax
import jax.numpy as jnp
from jax import lax
from jax.experimental import pallas as pl
from jax.experimental.pallas import tpu as pltpu
from jax.sharding import Mesh
from jax.sharding import PartitionSpec as P

ROPE = 64
NOPE = 128
NY, NZ, NC, NX = 4, 8, 2, 4
F32 = jnp.float32
BF16 = jnp.bfloat16
VMEM = pl.BlockSpec(memory_space=pltpu.VMEM)
ANY = pl.BlockSpec(memory_space=pl.ANY)
HBM = pl.BlockSpec(memory_space=pltpu.HBM)
SMEM = pl.BlockSpec(memory_space=pltpu.SMEM)
LARGE = pltpu.CompilerParams(vmem_limit_bytes=60 * 1024 * 1024)
SMALL = pltpu.CompilerParams(vmem_limit_bytes=16 * 1024 * 1024)


def dot(a, b):
    return jnp.dot(a, b, preferred_element_type=F32)


def dot_t(a, b):
    return lax.dot_general(a, b, (((1,), (1,)), ((), ())), preferred_element_type=F32)


def shift(n, k):
    return [(i, (i + k) % n) for i in range(n)]


def fetch(v, axis, n):
    return [v] + [lax.ppermute(v, axis, shift(n, -k)) for k in range(1, n)]


def ring(v, c, extras, other):
    blocks = [v] + [None] * (NZ - 1)
    up, down = v, v
    done = []
    for k in range(1, NZ // 2):
        up = lax.ppermute(up, "z", shift(NZ, 1))
        down = lax.ppermute(down, "z", shift(NZ, -1))
        blocks[NZ - k], blocks[k] = up, down
        done.append(other(lax.optimization_barrier((extras[k - 1], up))[0]))
    ways = [
        (i * NC + core, (i + way) % NZ * NC + core)
        for i in range(NZ)
        for core, way in ((0, 1), (1, NZ - 1))
    ]
    last = lax.ppermute(jnp.where(c == 0, up, down), ("z", "c"), ways)
    blocks[NZ // 2], done = lax.optimization_barrier((last, done))
    return blocks, done


def moved(rows, source):
    i = lax.broadcasted_iota(jnp.int32, (rows, rows), 0)
    j = lax.broadcasted_iota(jnp.int32, (rows, rows), 1)
    return (source(i) == j).astype(BF16)


def attend_kernel(scale, lengths, queries, new_entries, entries, w_uv, out, latents, cache, w, sems):
    count, entry, span = cache.shape
    steps, heads = queries.shape[1:3]
    latent = latents.shape[2]
    value = w.shape[2]
    loads = [pltpu.make_async_copy(entries.at[r], cache.at[r], sems.at[r]) for r in range(count)]
    loads.append(pltpu.make_async_copy(w_uv, w, sems.at[count]))
    for load in loads:
        load.start()
    for r in range(count):
        rows = queries[r].reshape(steps * heads, entry)
        fresh = new_entries[r].astype(F32)
        step = lax.broadcasted_iota(jnp.int32, (steps * heads, 1), 0) // heads
        late = []
        for n in range(steps):
            s = jnp.sum(rows.astype(F32) * fresh[n : n + 1, :], axis=1, keepdims=True) * scale
            late.append(jnp.where(step >= n, s, -1e30))
        loads[r].wait()
        scores = dot(rows, cache[r]) * scale
        valid = lax.broadcasted_iota(jnp.int32, scores.shape, 1) < lengths[r]
        scores = jnp.where(valid, scores, -1e30)
        top = jnp.max(scores, axis=1, keepdims=True)
        for s in late:
            top = jnp.maximum(top, s)
        weights = jnp.exp(scores - top)
        late = [jnp.exp(s - top) for s in late]
        share = 1.0 / (jnp.sum(weights, axis=1, keepdims=True) + sum(late))
        result = dot_t((weights * share).astype(BF16), cache[r, :latent, :])
        for n in range(steps):
            result = result + (late[n] * share).astype(BF16).astype(F32) * fresh[n : n + 1, :latent]
        result = result.astype(BF16).astype(F32)
        for t in range(steps):
            latents[:, r * steps + t, :] = result[t * heads : (t + 1) * heads]
    loads[count].wait()
    for h in range(heads):
        out[:, h * value : (h + 1) * value] = dot(latents[h].astype(BF16), w[h]).astype(BF16)


def attend(queries, new_entries, cache, lengths, w_uv):
    rolls, steps, heads, entry = queries.shape
    _, latent, value = w_uv.shape
    return pl.pallas_call(
        lambda *refs: attend_kernel((NOPE + ROPE) ** (-0.5), *refs),
        out_shape=jax.ShapeDtypeStruct((rolls * steps, heads * value), BF16),
        in_specs=[SMEM, VMEM, VMEM, HBM, HBM],
        out_specs=VMEM,
        scratch_shapes=[
            pltpu.VMEM((heads, rolls * steps, latent), F32),
            pltpu.VMEM(cache.shape, BF16),
            pltpu.VMEM(w_uv.shape, BF16),
            pltpu.SemaphoreType.DMA((rolls + 1,)),
        ],
        compiler_params=LARGE,
        name="attend",
    )(lengths, queries, new_entries, cache, w_uv)


def project_kernel(count, place, *refs):
    pieces, refs = refs[:count], refs[count:]
    (w_own, w_alien, hidden, hidden_alien), outs = refs[:4], refs[4 : 4 + NX]
    lhs, w, sems = refs[4 + NX :]
    y, z, c, x = place[0], place[1], place[2], place[3]
    cols = w_own.shape[0]
    loads = [
        pltpu.make_async_copy(
            v, w.at[pl.ds(pl.multiple_of(at * cols, 16), cols)], sems.at[count + n]
        )
        for n, (v, at) in enumerate(((w_own, c), (w_alien, 1 - c)))
    ]
    rows = pieces[0].shape[0]
    for n, piece in enumerate(pieces):
        loads.append(
            pltpu.make_async_copy(piece, lhs.at[pl.ds(n * rows, rows)], sems.at[n])
        )
    for load in loads:
        load.start()

    def stream(values):
        steps = values.shape[0] // cols
        i = lax.broadcasted_iota(jnp.int32, (outs[0].shape[0], values.shape[1]), 0)
        j = lax.broadcasted_iota(jnp.int32, (outs[0].shape[0], values.shape[1]), 1)
        here = (lax.shift_right_logical(i, 1) * NC + c) * NX + x == j
        total = 0.0
        for t in range(steps):
            chosen = (here & ((i & 1) == t)).astype(BF16)
            total = total + dot_t(chosen, values[t * cols : (t + 1) * cols])
        return total

    own, alien = stream(hidden), stream(hidden_alien)
    added = jnp.concatenate(
        [jnp.where(c == 0, own, alien), jnp.where(c == 0, alien, own)], axis=1
    )

    def source(i):
        roll = (lax.shift_right_logical(i, 6) + x) & 3
        zz = (lax.shift_right_logical(i, 1) + NZ - z) & 7
        yy = (lax.shift_right_logical(i, 4) + NY - y) & 3
        return zz * 32 + yy * 8 + roll * 2 + (i & 1)

    order = moved(lhs.shape[0], source)
    for load in loads:
        load.wait()
    part = dot_t(lhs[...], w[...]).astype(BF16)
    part = dot(order, part)
    size = outs[0].shape[0]
    outs[0][...] = (part[:size] + added).astype(BF16)
    for n in range(1, NX):
        outs[n][...] = part[n * size : (n + 1) * size].astype(BF16)


def project(place, pieces, weights, hidden):
    rows = sum(p.shape[0] for p in pieces)
    cols, depth = weights[0].shape
    return pl.pallas_call(
        lambda *refs: project_kernel(len(pieces), *refs),
        out_shape=[jax.ShapeDtypeStruct((rows // NX, NC * cols), BF16)] * NX,
        in_specs=[SMEM] + [ANY] * len(pieces) + [HBM] * NC + [VMEM] * NC,
        out_specs=[VMEM] * NX,
        scratch_shapes=[
            pltpu.VMEM((rows, depth), BF16),
            pltpu.VMEM((NC * cols, depth), BF16),
            pltpu.SemaphoreType.DMA((len(pieces) + NC,)),
        ],
        compiler_params=LARGE,
        name="project",
    )(place, *pieces, *weights, *hidden)


def gate_up_kernel(place, gain, blocks, w0, w1, w2, w3, o0, o1, o2, o3, scaled, w, sems):
    hid = w0.shape[0]
    loads = [
        pltpu.make_async_copy(v, w.at[pl.ds(n * hid, hid)], sems.at[n])
        for n, v in enumerate((w0, w1, w2, w3))
    ]
    for load in loads:
        load.start()
    ny, nz, rows, cols = blocks.shape
    x = place[3]
    squares = [0.0] * ny
    for b in range(nz):
        for k in range(ny):
            block = blocks[(x + k) & 3, b].astype(F32)
            squares[k] = squares[k] + jnp.sum(block * block, axis=1, keepdims=True)
            scaled[k * rows : (k + 1) * rows, b * cols : (b + 1) * cols] = (
                block * gain[b : b + 1, :]
            ).astype(BF16)
    outs = (o0, o1, o2, o3)
    for n in range(NC):
        for load in loads[2 * n : 2 * n + 2]:
            load.wait()
        total = dot_t(scaled[...], w[2 * n * hid : 2 * (n + 1) * hid]).astype(BF16)
        for k, out in enumerate(outs):
            out[:, 2 * n * hid : 2 * (n + 1) * hid] = total[k * rows : (k + 1) * rows]
    for k, out in enumerate(outs):
        out[:, 4 * hid :] = jnp.broadcast_to(squares[k].astype(BF16), (rows, 128))


def gate_up(place, gain, blocks, weights):
    ny, nz, rows, cols = blocks.shape
    hid, width = weights[0].shape
    return pl.pallas_call(
        gate_up_kernel,
        out_shape=[jax.ShapeDtypeStruct((rows, 4 * hid + 128), BF16)] * ny,
        in_specs=[SMEM] + [VMEM] * 2 + [HBM] * 4,
        out_specs=[VMEM] * ny,
        scratch_shapes=[
            pltpu.VMEM((ny * rows, width), BF16),
            pltpu.VMEM((4 * hid, width), BF16),
            pltpu.SemaphoreType.DMA((4,)),
        ],
        compiler_params=LARGE,
        name="gate_up",
    )(place, gain, blocks, *weights)


def activate_kernel(features, hid, m0, m1, m2, m3, act):
    both = (m0[...].astype(F32) + m1[...].astype(F32)) + (
        m2[...].astype(F32) + m3[...].astype(F32)
    )
    both = both[:, : 4 * hid] * lax.rsqrt(both[:, 4 * hid : 4 * hid + 1] / features + 1e-06)
    for n in range(NC):
        gate = both[:, 2 * n * hid : (2 * n + 1) * hid]
        up = both[:, (2 * n + 1) * hid : (2 * n + 2) * hid]
        act[:, n * hid : (n + 1) * hid] = (jax.nn.silu(gate) * up).astype(BF16)


def activate(messages, features, hid):
    return pl.pallas_call(
        lambda *refs: activate_kernel(features, hid, *refs),
        out_shape=jax.ShapeDtypeStruct((messages[0].shape[0], NC * hid), BF16),
        in_specs=[VMEM] * NX,
        out_specs=VMEM,
        compiler_params=SMALL,
        name="activate",
    )(*messages)


def down_kernel(place, a0, a1, a2, a3, w_own, w_alien, out, act, w, sems):
    hid = w_own.shape[0]
    loads = [
        pltpu.make_async_copy(v, w.at[pl.ds(n * hid, hid)], sems.at[n])
        for n, v in enumerate((w_own, w_alien))
    ]
    for load in loads:
        load.start()
    x = place[3]
    rows = a0.shape[0]
    for n, a in enumerate((a0, a1, a2, a3)):
        act[n * rows : (n + 1) * rows] = a[...]
    for load in loads:
        load.wait()
    total = dot(act[...], w[...]).astype(BF16)
    part = rows // NY
    for n in range(NX):
        for b in range(NY):
            start = n * rows + b * part
            out[b, (x + n) & 3] = total[start : start + part]


def down(place, blocks, weights):
    rows = blocks[0].shape[0]
    hid, width = weights[0].shape
    return pl.pallas_call(
        down_kernel,
        out_shape=jax.ShapeDtypeStruct((NY, NX, rows // NY, width), BF16),
        in_specs=[SMEM] + [VMEM] * NX + [HBM] * NC,
        out_specs=VMEM,
        scratch_shapes=[
            pltpu.VMEM((NX * rows, NC * hid), BF16),
            pltpu.VMEM((NC * hid, width), BF16),
            pltpu.SemaphoreType.DMA((NC,)),
        ],
        compiler_params=SMALL,
        name="down",
    )(place, *blocks, *weights)


def sum_y_kernel(parts, out):
    total = parts[0].astype(F32)
    for n in range(1, NY):
        total = total + parts[n].astype(F32)

    def source(i):
        return (
            (lax.shift_right_logical(i, 1) & 3) * 16 + lax.shift_right_logical(i, 3) * 2 + (i & 1)
        )

    out[...] = dot(moved(out.shape[0], source), total.astype(BF16)).astype(BF16)


def sum_y(parts):
    return pl.pallas_call(
        sum_y_kernel,
        out_shape=jax.ShapeDtypeStruct(parts.shape[1:], BF16),
        in_specs=[VMEM],
        out_specs=VMEM,
        compiler_params=SMALL,
        name="sum_y",
    )(parts)


def on_device(
    queries, new_entries, cache, lengths, hidden, w_uv, w_o, ffn_gain, w_gate, w_up, w_down
):
    y, z, c, x = (lax.axis_index(a) for a in ("y", "z", "c", "x"))
    place = jnp.stack([y, z, c, x]).astype(jnp.int32)
    rolls, steps = queries.shape[:2]
    pair = NC * w_o.shape[1]
    width, hid = w_gate.shape
    cache = cache.transpose(0, 2, 1)
    hidden = hidden.transpose(1, 2, 0).reshape(-1, hidden.shape[0])
    w_o, w_gate, w_up = w_o.T, w_gate.T, w_up.T

    def other(v):
        return lax.ppermute(v, "c", shift(NC, 1))

    def cross(v, k):
        return lax.ppermute(
            v, ("y", "x"), [(b * NX + a, ((a + k) % NX) * NX + b) for b in range(NY) for a in range(NX)]
        )

    with jax.named_scope("attend"):
        w_o_alien, hidden_alien = other(w_o), other(hidden)
        head_out = attend(queries, new_entries, cache, lengths, w_uv)
        head_out, w_o_alien, hidden_alien = lax.optimization_barrier(
            (head_out, w_o_alien, hidden_alien)
        )

    with jax.named_scope("gather_heads"):
        near = jnp.concatenate(fetch(head_out, "y", NY), axis=0)
        pieces, swapped = ring(near, c, (w_gate, w_up, w_down), other)
        w_gate_alien, w_up_alien, w_down_alien = swapped

    with jax.named_scope("project"):
        parts = project(place, pieces, (w_o, w_o_alien), (hidden, hidden_alien))

    with jax.named_scope("sum_heads"):
        total = 0.0
        for k in range(NX):
            total = total + cross(parts[k], k).astype(F32)
        resid = total.astype(BF16)

    with jax.named_scope("gather_resid"):
        resid = lax.all_to_all(jnp.broadcast_to(resid[None], (NZ,) + resid.shape), "z", 0, 0)
        resid = lax.all_gather(resid, "y")

    with jax.named_scope("gate_up"):
        gain = lax.dynamic_slice_in_dim(ffn_gain, x * width, width, 0).astype(F32)
        messages = gate_up(
            place, gain.reshape(NZ, pair), resid, (w_gate, w_up, w_gate_alien, w_up_alien)
        )

    with jax.named_scope("sum_gate_up"):
        messages = [messages[0]] + [
            lax.ppermute(messages[k], "x", shift(NX, k)) for k in range(1, NX)
        ]
        act = activate(messages, NX * width, hid)

    with jax.named_scope("down"):
        out = down(place, fetch(act, "x", NX), (w_down, w_down_alien))

    with jax.named_scope("sum_y"):
        out = lax.all_to_all(out.reshape(NY, -1, width), "y", 0, 0)
        out = sum_y(out)

    with jax.named_scope("sum_z"):
        out = lax.all_to_all(out.reshape(NZ, rolls * steps, width), "z", 0, 0)
        out = jnp.sum(out.astype(F32), axis=0)

    with jax.named_scope("finish"):
        own = lax.dynamic_slice_in_dim(resid, (y * NZ + z) * steps, steps, 2)
        own = own.transpose(0, 2, 1, 3).reshape(rolls * steps, width)
        out = (own.astype(F32) + out).astype(BF16)
    return out.reshape(rolls, steps, width)


def solution(mesh):
    fine = Mesh(mesh.devices.reshape(NY, NZ, NC, NX), ("y", "z", "c", "x"))
    dp = ("y", "z", "c")
    placed = (
        P(dp, None, "x", None),
        P(dp, None, None),
        P(dp, None, None),
        P(dp),
        P(None, None, dp),
        P("x", None, None),
        P("x", dp),
        P(),
        P("x", dp),
        P("x", dp),
        P(dp, "x"),
    )
    return jax.shard_map(
        on_device, mesh=fine, in_specs=placed, out_specs=P(dp, None, "x"), check_vma=False
    )
```

```python
import jax
import jax.numpy as jnp
from jax import lax
from jax.experimental import pallas as pl
from jax.experimental.pallas import tpu as pltpu
from jax.sharding import Mesh
from jax.sharding import PartitionSpec as P

ROPE = 64
NOPE = 128
NY, NZ, NC, NX = 4, 8, 2, 4
F32 = jnp.float32
BF16 = jnp.bfloat16
VMEM = pl.BlockSpec(memory_space=pltpu.VMEM)
ANY = pl.BlockSpec(memory_space=pl.ANY)
HBM = pl.BlockSpec(memory_space=pltpu.HBM)
SMEM = pl.BlockSpec(memory_space=pltpu.SMEM)
LARGE = pltpu.CompilerParams(vmem_limit_bytes=52 * 1024 * 1024)
ATT = pltpu.CompilerParams(vmem_limit_bytes=60 * 1024 * 1024)
CUT = pltpu.CompilerParams(vmem_limit_bytes=60 * 1024 * 1024)
SMALL = pltpu.CompilerParams(vmem_limit_bytes=16 * 1024 * 1024)


def dot(a, b):
    return jnp.dot(a, b, preferred_element_type=F32)


def dot_t(a, b):
    return lax.dot_general(a, b, (((1,), (1,)), ((), ())), preferred_element_type=F32)


def shift(n, k):
    return [(i, (i + k) % n) for i in range(n)]


def fetch(v, axis, n):
    return [v] + [lax.ppermute(v, axis, shift(n, -k)) for k in range(1, n)]


def spread(v, axis, n):
    return lax.all_to_all(jnp.broadcast_to(v[None], (n,) + v.shape), axis, 0, 0)


def moved(rows, source):
    i = lax.broadcasted_iota(jnp.int32, (rows, rows), 0)
    j = lax.broadcasted_iota(jnp.int32, (rows, rows), 1)
    return (source(i) == j).astype(BF16)


def attend_kernel(
    scale, lengths, q, new_entries, entries, w_uv, out, queries, latents, cache, w, sems
):
    count, entry, span = cache.shape
    steps, heads = queries.shape[1:3]
    latent = latents.shape[2]
    value = w.shape[2]
    loads = [pltpu.make_async_copy(entries.at[r], cache.at[r], sems.at[r]) for r in range(count)]
    loads.append(pltpu.make_async_copy(w_uv, w, sems.at[count]))
    first = pltpu.make_async_copy(q, queries, sems.at[count + 1])
    first.start()
    for load in loads:
        load.start()
    first.wait()
    for r in range(count):
        rows = queries[r].reshape(steps * heads, entry)
        fresh = new_entries[r].astype(F32)
        step = lax.broadcasted_iota(jnp.int32, (steps * heads, 1), 0) // heads
        late = []
        for n in range(steps):
            s = jnp.sum(rows.astype(F32) * fresh[n : n + 1, :], axis=1, keepdims=True) * scale
            late.append(jnp.where(step >= n, s, -1e30))
        loads[r].wait()
        scores = dot(rows, cache[r]) * scale
        valid = lax.broadcasted_iota(jnp.int32, scores.shape, 1) < lengths[r]
        scores = jnp.where(valid, scores, -1e30)
        top = jnp.max(scores, axis=1, keepdims=True)
        for s in late:
            top = jnp.maximum(top, s)
        weights = jnp.exp(scores - top)
        late = [jnp.exp(s - top) for s in late]
        share = 1.0 / (jnp.sum(weights, axis=1, keepdims=True) + sum(late))
        result = dot_t((weights * share).astype(BF16), cache[r, :latent, :])
        for n in range(steps):
            result = result + (late[n] * share).astype(BF16).astype(F32) * fresh[n : n + 1, :latent]
        result = result.astype(BF16).astype(F32)
        for t in range(steps):
            latents[:, r * steps + t, :] = result[t * heads : (t + 1) * heads]
    loads[count].wait()
    for h in range(heads):
        part, n = divmod(h, heads // NY)
        result = dot(latents[h].astype(BF16), w[h]).astype(BF16)
        for b in range(NZ):
            out[part, b, :, n * value : (n + 1) * value] = result


def attend(queries, new_entries, cache, lengths, w_uv):
    rolls, steps, heads, entry = queries.shape
    _, latent, value = w_uv.shape
    return pl.pallas_call(
        lambda *refs: attend_kernel((NOPE + ROPE) ** (-0.5), *refs),
        out_shape=jax.ShapeDtypeStruct((NY, NZ, rolls * steps, heads * value // NY), BF16),
        in_specs=[SMEM, HBM, VMEM, HBM, HBM],
        out_specs=VMEM,
        scratch_shapes=[
            pltpu.VMEM(queries.shape, BF16),
            pltpu.VMEM((heads, rolls * steps, latent), F32),
            pltpu.VMEM(cache.shape, BF16),
            pltpu.VMEM(w_uv.shape, BF16),
            pltpu.SemaphoreType.DMA((rolls + 2,)),
        ],
        compiler_params=ATT,
        name="attend",
    )(lengths, queries, new_entries, cache, w_uv)


def cut_kernel(v, out, sems):
    blocks, _, depth = out.shape
    moves = [
        pltpu.make_async_copy(v.at[:, b * depth : (b + 1) * depth], out.at[b], sems.at[b])
        for b in range(blocks)
    ]
    for move in moves:
        move.start()
    for move in moves:
        move.wait()


def cut(v, blocks):
    rows, width = v.shape
    return pl.pallas_call(
        cut_kernel,
        out_shape=jax.ShapeDtypeStruct((blocks, rows, width // blocks), v.dtype),
        in_specs=[HBM],
        out_specs=VMEM,
        scratch_shapes=[pltpu.SemaphoreType.DMA((blocks,))],
        compiler_params=CUT,
        name="cut",
    )(v)


def project_kernel(place, lhs_in, w_own, w_alien, hidden, hidden_alien, out, lhs, w, sems):
    y, z, c, x = place[0], place[1], place[2], place[3]
    blocks, cols = w_own.shape[:2]
    loads = [pltpu.make_async_copy(lhs_in, lhs, sems.at[0])]
    for n, (v, at) in enumerate(((w_own, c), (w_alien, 1 - c))):
        for b in range(blocks):
            to = pl.multiple_of((b * NC + at) * cols, 16)
            loads.append(
                pltpu.make_async_copy(v.at[b], w.at[pl.ds(to, cols)], sems.at[1 + n * blocks + b])
            )
    for load in loads:
        load.start()
    rows, size = lhs.shape[0], out.shape[1]

    def stream(values):
        steps = values.shape[0] // cols
        i = lax.broadcasted_iota(jnp.int32, (size, values.shape[1]), 0)
        j = lax.broadcasted_iota(jnp.int32, (size, values.shape[1]), 1)
        here = (lax.shift_right_logical(i, 1) * NC + c) * NX + x == j
        total = 0.0
        for t in range(steps):
            chosen = (here & ((i & 1) == t)).astype(BF16)
            total = total + dot_t(chosen, values[t * cols : (t + 1) * cols])
        return total

    own, alien = stream(hidden), stream(hidden_alien)
    added = jnp.concatenate(
        [jnp.where(c == 0, own, alien), jnp.where(c == 0, alien, own)], axis=1
    )

    def source(i):
        roll = lax.shift_right_logical(i, 6)
        zz = lax.shift_right_logical(i, 1) & 7
        yy = lax.shift_right_logical(i, 4) & 3
        return yy * 64 + zz * 8 + roll * 2 + (i & 1)

    order = moved(rows, source)
    for load in loads:
        load.wait()
    pair = NC * cols
    for b in range(blocks):
        part = dot_t(lhs[...], w[b * pair : (b + 1) * pair]).astype(BF16)
        part = dot(order, part)
        for j in range(NX):
            piece = part[j * size : (j + 1) * size]
            piece = piece + jnp.where((j == x) & (b == y), added, 0.0)
            out[j * blocks + b] = piece.astype(BF16)


def project(place, lhs, weights, hidden):
    rows, depth = lhs.shape
    blocks, cols, _ = weights[0].shape
    return pl.pallas_call(
        project_kernel,
        out_shape=jax.ShapeDtypeStruct((NX * blocks, rows // NX, NC * cols), BF16),
        in_specs=[SMEM, ANY] + [HBM] * NC + [VMEM] * NC,
        out_specs=VMEM,
        scratch_shapes=[
            pltpu.VMEM((rows, depth), BF16),
            pltpu.VMEM((blocks * NC * cols, depth), BF16),
            pltpu.SemaphoreType.DMA((1 + NC * blocks,)),
        ],
        compiler_params=SMALL,
        name="project",
    )(place, lhs, *weights, *hidden)


def gate_up_kernel(
    place, gain, blocks_in, w0, w1, w2, w3, o0, o1, o2, o3, blocks, scaled, w, sems
):
    hid = w0.shape[0]
    loads = [
        pltpu.make_async_copy(v, w.at[pl.ds(n * hid, hid)], sems.at[n])
        for n, v in enumerate((w0, w1, w2, w3))
    ]
    first = pltpu.make_async_copy(blocks_in, blocks, sems.at[4])
    first.start()
    for load in loads:
        load.start()
    ny, nz, rows, cols = blocks.shape
    x = place[3]
    squares = [0.0] * ny
    first.wait()
    for b in range(nz):
        for k in range(ny):
            block = blocks[(x + k) & 3, b].astype(F32)
            squares[k] = squares[k] + jnp.sum(block * block, axis=1, keepdims=True)
            scaled[k * rows : (k + 1) * rows, b * cols : (b + 1) * cols] = (
                block * gain[b : b + 1, :]
            ).astype(BF16)
    outs = (o0, o1, o2, o3)
    for n in range(NC):
        for load in loads[2 * n : 2 * n + 2]:
            load.wait()
        total = dot_t(scaled[...], w[2 * n * hid : 2 * (n + 1) * hid]).astype(BF16)
        for k, out in enumerate(outs):
            out[:, 2 * n * hid : 2 * (n + 1) * hid] = total[k * rows : (k + 1) * rows]
    for k, out in enumerate(outs):
        out[:, 4 * hid :] = jnp.broadcast_to(squares[k].astype(BF16), (rows, 128))


def gate_up(place, gain, blocks, weights):
    ny, nz, rows, cols = blocks.shape
    hid, width = weights[0].shape
    return pl.pallas_call(
        gate_up_kernel,
        out_shape=[jax.ShapeDtypeStruct((rows, 4 * hid + 128), BF16)] * ny,
        in_specs=[SMEM, VMEM, ANY] + [HBM] * 4,
        out_specs=[VMEM] * ny,
        scratch_shapes=[
            pltpu.VMEM(blocks.shape, BF16),
            pltpu.VMEM((ny * rows, width), BF16),
            pltpu.VMEM((4 * hid, width), BF16),
            pltpu.SemaphoreType.DMA((5,)),
        ],
        compiler_params=LARGE,
        name="gate_up",
    )(place, gain, blocks, *weights)


def activate_kernel(features, hid, m0, m1, m2, m3, act):
    both = (m0[...].astype(F32) + m1[...].astype(F32)) + (
        m2[...].astype(F32) + m3[...].astype(F32)
    )
    both = both[:, : 4 * hid] * lax.rsqrt(both[:, 4 * hid : 4 * hid + 1] / features + 1e-06)
    for n in range(NC):
        gate = both[:, 2 * n * hid : (2 * n + 1) * hid]
        up = both[:, (2 * n + 1) * hid : (2 * n + 2) * hid]
        act[:, n * hid : (n + 1) * hid] = (jax.nn.silu(gate) * up).astype(BF16)


def activate(messages, features, hid):
    return pl.pallas_call(
        lambda *refs: activate_kernel(features, hid, *refs),
        out_shape=jax.ShapeDtypeStruct((messages[0].shape[0], NC * hid), BF16),
        in_specs=[VMEM] * NX,
        out_specs=VMEM,
        compiler_params=SMALL,
        name="activate",
    )(*messages)


def down_kernel(place, a0, a1, a2, a3, w_own, w_alien, out, act, w, sems):
    hid = w_own.shape[0]
    loads = [
        pltpu.make_async_copy(v, w.at[pl.ds(n * hid, hid)], sems.at[n])
        for n, v in enumerate((w_own, w_alien))
    ]
    for load in loads:
        load.start()
    x = place[3]
    rows = a0.shape[0]
    for n, a in enumerate((a0, a1, a2, a3)):
        act[n * rows : (n + 1) * rows] = a[...]
    for load in loads:
        load.wait()
    total = dot(act[...], w[...]).astype(BF16)
    part = rows // NY
    for n in range(NX):
        for b in range(NY):
            start = n * rows + b * part
            out[b, (x + n) & 3] = total[start : start + part]


def down(place, blocks, weights):
    rows = blocks[0].shape[0]
    hid, width = weights[0].shape
    return pl.pallas_call(
        down_kernel,
        out_shape=jax.ShapeDtypeStruct((NY, NX, rows // NY, width), BF16),
        in_specs=[SMEM] + [VMEM] * NX + [HBM] * NC,
        out_specs=VMEM,
        scratch_shapes=[
            pltpu.VMEM((NX * rows, NC * hid), BF16),
            pltpu.VMEM((NC * hid, width), BF16),
            pltpu.SemaphoreType.DMA((NC,)),
        ],
        compiler_params=SMALL,
        name="down",
    )(place, *blocks, *weights)


def sum_y_kernel(parts, out):
    total = parts[0].astype(F32)
    for n in range(1, NY):
        total = total + parts[n].astype(F32)

    def source(i):
        return (
            (lax.shift_right_logical(i, 1) & 3) * 16 + lax.shift_right_logical(i, 3) * 2 + (i & 1)
        )

    out[...] = dot(moved(out.shape[0], source), total.astype(BF16)).astype(BF16)


def sum_y(parts):
    return pl.pallas_call(
        sum_y_kernel,
        out_shape=jax.ShapeDtypeStruct(parts.shape[1:], BF16),
        in_specs=[VMEM],
        out_specs=VMEM,
        compiler_params=SMALL,
        name="sum_y",
    )(parts)


def on_device(
    queries, new_entries, cache, lengths, hidden, w_uv, w_o, ffn_gain, w_gate, w_up, w_down
):
    y, z, c, x = (lax.axis_index(a) for a in ("y", "z", "c", "x"))
    place = jnp.stack([y, z, c, x]).astype(jnp.int32)
    rolls, steps = queries.shape[:2]
    pair = NC * w_o.shape[1]
    width, hid = w_gate.shape
    cache = cache.transpose(0, 2, 1)
    hidden = hidden.transpose(1, 2, 0).reshape(-1, hidden.shape[0])
    w_o, w_gate, w_up = w_o.T, w_gate.T, w_up.T

    def other(v):
        return lax.ppermute(v, "c", shift(NC, 1))

    with jax.named_scope("attend"):
        depth = w_o.shape[1] // NY
        w_o = lax.all_to_all(cut(w_o, NY), "y", 0, 0)
        swapped = [other(v) for v in (hidden, w_gate, w_up, w_down)]
        head_out = attend(queries, new_entries, cache, lengths, w_uv)
        head_out, w_o, swapped = lax.optimization_barrier((head_out, w_o, swapped))
        hidden_alien, w_gate_alien, w_up_alien, w_down_alien = swapped

    with jax.named_scope("gather_heads"):
        w_o_alien = other(w_o)
        near = lax.all_to_all(head_out.reshape(NY * NZ, -1, depth), ("y", "z"), 0, 0)
        near, w_o_alien = lax.optimization_barrier((near, w_o_alien))

    with jax.named_scope("project"):
        parts = project(
            place, near.reshape(-1, depth), (w_o, w_o_alien), (hidden, hidden_alien)
        )

    with jax.named_scope("sum_heads"):
        parts = lax.all_to_all(parts, ("y", "x"), 0, 0)
        resid = jnp.sum(parts.astype(F32), axis=0).astype(BF16)

    with jax.named_scope("gather_resid"):
        resid = spread(resid, "z", NZ)
        resid = lax.all_gather(resid, "y")

    with jax.named_scope("gate_up"):
        gain = lax.dynamic_slice_in_dim(ffn_gain, x * width, width, 0).astype(F32)
        messages = gate_up(
            place, gain.reshape(NZ, pair), resid, (w_gate, w_up, w_gate_alien, w_up_alien)
        )

    with jax.named_scope("sum_gate_up"):
        messages = [messages[0]] + [
            lax.ppermute(messages[k], "x", shift(NX, k)) for k in range(1, NX)
        ]
        act = activate(messages, NX * width, hid)

    with jax.named_scope("down"):
        out = down(place, fetch(act, "x", NX), (w_down, w_down_alien))

    with jax.named_scope("sum_y"):
        out = lax.all_to_all(out.reshape(NY, -1, width), "y", 0, 0)
        out = sum_y(out)

    with jax.named_scope("sum_z"):
        out = lax.all_to_all(out.reshape(NZ, rolls * steps, width), "z", 0, 0)
        out = jnp.sum(out.astype(F32), axis=0)

    with jax.named_scope("finish"):
        own = lax.dynamic_slice_in_dim(resid, (y * NZ + z) * steps, steps, 2)
        own = own.transpose(0, 2, 1, 3).reshape(rolls * steps, width)
        out = (own.astype(F32) + out).astype(BF16)
    return out.reshape(rolls, steps, width)


def solution(mesh):
    fine = Mesh(mesh.devices.reshape(NY, NZ, NC, NX), ("y", "z", "c", "x"))
    dp = ("y", "z", "c")
    placed = (
        P(dp, None, "x", None),
        P(dp, None, None),
        P(dp, None, None),
        P(dp),
        P(None, None, dp),
        P("x", None, None),
        P("x", dp),
        P(),
        P("x", dp),
        P("x", dp),
        P(dp, "x"),
    )
    return jax.shard_map(
        on_device, mesh=fine, in_specs=placed, out_specs=P(dp, None, "x"), check_vma=False
    )
```

```python
import jax
import jax.numpy as jnp
from jax import lax
from jax.experimental import pallas as pl
from jax.experimental.pallas import tpu as pltpu
from jax.sharding import Mesh
from jax.sharding import PartitionSpec as P

ROPE = 64
NOPE = 128
NY, NZ, NC, NX = 4, 8, 2, 4
F32 = jnp.float32
BF16 = jnp.bfloat16
VMEM = pl.BlockSpec(memory_space=pltpu.VMEM)
ANY = pl.BlockSpec(memory_space=pl.ANY)
HBM = pl.BlockSpec(memory_space=pltpu.HBM)
SMEM = pl.BlockSpec(memory_space=pltpu.SMEM)
LARGE = pltpu.CompilerParams(vmem_limit_bytes=52 * 1024 * 1024)
ATT = pltpu.CompilerParams(vmem_limit_bytes=60 * 1024 * 1024)
CUT = pltpu.CompilerParams(vmem_limit_bytes=60 * 1024 * 1024)
SMALL = pltpu.CompilerParams(vmem_limit_bytes=16 * 1024 * 1024)


def dot(a, b):
    return jnp.dot(a, b, preferred_element_type=F32)


def dot_t(a, b):
    return lax.dot_general(a, b, (((1,), (1,)), ((), ())), preferred_element_type=F32)


def shift(n, k):
    return [(i, (i + k) % n) for i in range(n)]


def fetch(v, axis, n):
    return [v] + [lax.ppermute(v, axis, shift(n, -k)) for k in range(1, n)]


def moved(rows, source):
    i = lax.broadcasted_iota(jnp.int32, (rows, rows), 0)
    j = lax.broadcasted_iota(jnp.int32, (rows, rows), 1)
    return (source(i) == j).astype(BF16)


def attend_kernel(
    scale, lengths, q, new_entries, entries, w_uv, out, queries, latents, cache, w, sems
):
    count, entry, span = cache.shape
    steps, heads = queries.shape[1:3]
    latent = latents.shape[2]
    value = w.shape[2]
    loads = [pltpu.make_async_copy(entries.at[r], cache.at[r], sems.at[r]) for r in range(count)]
    loads.append(pltpu.make_async_copy(w_uv, w, sems.at[count]))
    first = pltpu.make_async_copy(q, queries, sems.at[count + 1])
    first.start()
    for load in loads:
        load.start()
    first.wait()
    for r in range(count):
        rows = queries[r].reshape(steps * heads, entry)
        fresh = new_entries[r].astype(F32)
        step = lax.broadcasted_iota(jnp.int32, (steps * heads, 1), 0) // heads
        late = []
        for n in range(steps):
            s = jnp.sum(rows.astype(F32) * fresh[n : n + 1, :], axis=1, keepdims=True) * scale
            late.append(jnp.where(step >= n, s, -1e30))
        loads[r].wait()
        scores = dot(rows, cache[r]) * scale
        valid = lax.broadcasted_iota(jnp.int32, scores.shape, 1) < lengths[r]
        scores = jnp.where(valid, scores, -1e30)
        top = jnp.max(scores, axis=1, keepdims=True)
        for s in late:
            top = jnp.maximum(top, s)
        weights = jnp.exp(scores - top)
        late = [jnp.exp(s - top) for s in late]
        share = 1.0 / (jnp.sum(weights, axis=1, keepdims=True) + sum(late))
        result = dot_t((weights * share).astype(BF16), cache[r, :latent, :])
        for n in range(steps):
            result = result + (late[n] * share).astype(BF16).astype(F32) * fresh[n : n + 1, :latent]
        result = result.astype(BF16).astype(F32)
        for t in range(steps):
            latents[:, r * steps + t, :] = result[t * heads : (t + 1) * heads]
    loads[count].wait()
    for h in range(heads):
        part, n = divmod(h, heads // NY)
        result = dot(latents[h].astype(BF16), w[h]).astype(BF16)
        for b in range(NZ):
            out[part, b, :, n * value : (n + 1) * value] = result


def attend(queries, new_entries, cache, lengths, w_uv):
    rolls, steps, heads, entry = queries.shape
    _, latent, value = w_uv.shape
    return pl.pallas_call(
        lambda *refs: attend_kernel((NOPE + ROPE) ** (-0.5), *refs),
        out_shape=jax.ShapeDtypeStruct((NY, NZ, rolls * steps, heads * value // NY), BF16),
        in_specs=[SMEM, HBM, VMEM, HBM, HBM],
        out_specs=VMEM,
        scratch_shapes=[
            pltpu.VMEM(queries.shape, BF16),
            pltpu.VMEM((heads, rolls * steps, latent), F32),
            pltpu.VMEM(cache.shape, BF16),
            pltpu.VMEM(w_uv.shape, BF16),
            pltpu.SemaphoreType.DMA((rolls + 2,)),
        ],
        compiler_params=ATT,
        name="attend",
    )(lengths, queries, new_entries, cache, w_uv)


def cut_kernel(v, out, sems):
    blocks, _, depth = out.shape
    moves = [
        pltpu.make_async_copy(v.at[:, b * depth : (b + 1) * depth], out.at[b], sems.at[b])
        for b in range(blocks)
    ]
    for move in moves:
        move.start()
    for move in moves:
        move.wait()


def cut(v, blocks):
    rows, width = v.shape
    return pl.pallas_call(
        cut_kernel,
        out_shape=jax.ShapeDtypeStruct((blocks, rows, width // blocks), v.dtype),
        in_specs=[HBM],
        out_specs=VMEM,
        scratch_shapes=[pltpu.SemaphoreType.DMA((blocks,))],
        compiler_params=CUT,
        name="cut",
    )(v)


def stream_kernel(steps, place, hidden, hidden_alien, out):
    c, x = place[2], place[3]
    size = out.shape[0]

    def chosen(values):
        cols = values.shape[0] // steps
        i = lax.broadcasted_iota(jnp.int32, (size, values.shape[1]), 0)
        j = lax.broadcasted_iota(jnp.int32, (size, values.shape[1]), 1)
        here = (lax.shift_right_logical(i, 1) * NC + c) * NX + x == j
        total = 0.0
        for t in range(steps):
            rows = (here & ((i & 1) == t)).astype(BF16)
            total = total + dot_t(rows, values[t * cols : (t + 1) * cols])
        return total

    own, alien = chosen(hidden), chosen(hidden_alien)
    out[...] = jnp.concatenate(
        [jnp.where(c == 0, own, alien), jnp.where(c == 0, alien, own)], axis=1
    ).astype(BF16)


def stream(place, hidden, hidden_alien, steps):
    rows = NY * NZ * steps
    return pl.pallas_call(
        lambda *refs: stream_kernel(steps, *refs),
        out_shape=jax.ShapeDtypeStruct((rows, NC * hidden.shape[0] // steps), BF16),
        in_specs=[SMEM, VMEM, VMEM],
        out_specs=VMEM,
        compiler_params=SMALL,
        name="stream",
    )(place, hidden, hidden_alien)


def project_kernel(place, lhs_in, w_own, w_alien, added, out, lhs, w, sems):
    y, z, c, x = place[0], place[1], place[2], place[3]
    blocks, cols = w_own.shape[:2]
    loads = [pltpu.make_async_copy(lhs_in, lhs, sems.at[0])]
    for n, (v, at) in enumerate(((w_own, c), (w_alien, 1 - c))):
        for b in range(blocks):
            to = pl.multiple_of((b * NC + at) * cols, 16)
            loads.append(
                pltpu.make_async_copy(v.at[b], w.at[pl.ds(to, cols)], sems.at[1 + n * blocks + b])
            )
    for load in loads:
        load.start()
    rows, size = lhs.shape[0], out.shape[1]

    def source(i):
        roll = lax.shift_right_logical(i, 6)
        zz = lax.shift_right_logical(i, 1) & 7
        yy = lax.shift_right_logical(i, 4) & 3
        return yy * 64 + zz * 8 + roll * 2 + (i & 1)

    order = moved(rows, source)
    for load in loads:
        load.wait()
    pair = NC * cols
    for b in range(blocks):
        part = dot_t(lhs[...], w[b * pair : (b + 1) * pair]).astype(BF16)
        part = dot(order, part)
        for j in range(NX):
            piece = part[j * size : (j + 1) * size]
            piece = piece + jnp.where((j == x) & (b == y), added[...].astype(F32), 0.0)
            out[j * blocks + b] = piece.astype(BF16)


def project(place, lhs, weights, added):
    rows, depth = lhs.shape
    blocks, cols, _ = weights[0].shape
    return pl.pallas_call(
        project_kernel,
        out_shape=jax.ShapeDtypeStruct((NX * blocks, rows // NX, NC * cols), BF16),
        in_specs=[SMEM, ANY] + [HBM] * NC + [VMEM],
        out_specs=VMEM,
        scratch_shapes=[
            pltpu.VMEM((rows, depth), BF16),
            pltpu.VMEM((blocks * NC * cols, depth), BF16),
            pltpu.SemaphoreType.DMA((1 + NC * blocks,)),
        ],
        compiler_params=SMALL,
        name="project",
    )(place, lhs, *weights, added)


def sum_heads_kernel(parts, out):
    total = parts[0].astype(F32)
    for n in range(1, parts.shape[0]):
        total = total + parts[n].astype(F32)
    for b in range(out.shape[0]):
        out[b] = total.astype(BF16)


def sum_heads(parts):
    return pl.pallas_call(
        sum_heads_kernel,
        out_shape=jax.ShapeDtypeStruct((NZ,) + parts.shape[1:], BF16),
        in_specs=[VMEM],
        out_specs=VMEM,
        compiler_params=SMALL,
        name="sum_heads",
    )(parts)


def gate_up_kernel(
    place, gain, blocks_in, w0, w1, w2, w3, o0, o1, o2, o3, blocks, scaled, w, sems
):
    hid = w0.shape[0]
    loads = [
        pltpu.make_async_copy(v, w.at[pl.ds(n * hid, hid)], sems.at[n])
        for n, v in enumerate((w0, w1, w2, w3))
    ]
    first = pltpu.make_async_copy(blocks_in, blocks, sems.at[4])
    first.start()
    for load in loads:
        load.start()
    ny, nz, rows, cols = blocks.shape
    x = place[3]
    squares = [0.0] * ny
    first.wait()
    for b in range(nz):
        for k in range(ny):
            block = blocks[(x + k) & 3, b].astype(F32)
            squares[k] = squares[k] + jnp.sum(block * block, axis=1, keepdims=True)
            scaled[k * rows : (k + 1) * rows, b * cols : (b + 1) * cols] = (
                block * gain[b : b + 1, :]
            ).astype(BF16)
    outs = (o0, o1, o2, o3)
    for n in range(NC):
        for load in loads[2 * n : 2 * n + 2]:
            load.wait()
        total = dot_t(scaled[...], w[2 * n * hid : 2 * (n + 1) * hid]).astype(BF16)
        for k, out in enumerate(outs):
            out[:, 2 * n * hid : 2 * (n + 1) * hid] = total[k * rows : (k + 1) * rows]
    for k, out in enumerate(outs):
        out[:, 4 * hid :] = jnp.broadcast_to(squares[k].astype(BF16), (rows, 128))


def gate_up(place, gain, blocks, weights):
    ny, nz, rows, cols = blocks.shape
    hid, width = weights[0].shape
    return pl.pallas_call(
        gate_up_kernel,
        out_shape=[jax.ShapeDtypeStruct((rows, 4 * hid + 128), BF16)] * ny,
        in_specs=[SMEM, VMEM, ANY] + [HBM] * 4,
        out_specs=[VMEM] * ny,
        scratch_shapes=[
            pltpu.VMEM(blocks.shape, BF16),
            pltpu.VMEM((ny * rows, width), BF16),
            pltpu.VMEM((4 * hid, width), BF16),
            pltpu.SemaphoreType.DMA((5,)),
        ],
        compiler_params=LARGE,
        name="gate_up",
    )(place, gain, blocks, *weights)


def activate_kernel(features, hid, m0, m1, m2, m3, act):
    both = (m0[...].astype(F32) + m1[...].astype(F32)) + (
        m2[...].astype(F32) + m3[...].astype(F32)
    )
    both = both[:, : 4 * hid] * lax.rsqrt(both[:, 4 * hid : 4 * hid + 1] / features + 1e-06)
    for n in range(NC):
        gate = both[:, 2 * n * hid : (2 * n + 1) * hid]
        up = both[:, (2 * n + 1) * hid : (2 * n + 2) * hid]
        act[:, n * hid : (n + 1) * hid] = (jax.nn.silu(gate) * up).astype(BF16)


def activate(messages, features, hid):
    return pl.pallas_call(
        lambda *refs: activate_kernel(features, hid, *refs),
        out_shape=jax.ShapeDtypeStruct((messages[0].shape[0], NC * hid), BF16),
        in_specs=[VMEM] * NX,
        out_specs=VMEM,
        compiler_params=SMALL,
        name="activate",
    )(*messages)


def down_kernel(place, a0, a1, a2, a3, w_own, w_alien, out, act, w, sems):
    hid = w_own.shape[0]
    loads = [
        pltpu.make_async_copy(v, w.at[pl.ds(n * hid, hid)], sems.at[n])
        for n, v in enumerate((w_own, w_alien))
    ]
    for load in loads:
        load.start()
    x = place[3]
    rows = a0.shape[0]
    for n, a in enumerate((a0, a1, a2, a3)):
        act[n * rows : (n + 1) * rows] = a[...]
    for load in loads:
        load.wait()
    total = dot(act[...], w[...]).astype(BF16)
    part = rows // NY
    for n in range(NX):
        for b in range(NY):
            start = n * rows + b * part
            out[b, (x + n) & 3] = total[start : start + part]


def down(place, blocks, weights):
    rows = blocks[0].shape[0]
    hid, width = weights[0].shape
    return pl.pallas_call(
        down_kernel,
        out_shape=jax.ShapeDtypeStruct((NY, NX, rows // NY, width), BF16),
        in_specs=[SMEM] + [VMEM] * NX + [HBM] * NC,
        out_specs=VMEM,
        scratch_shapes=[
            pltpu.VMEM((NX * rows, NC * hid), BF16),
            pltpu.VMEM((NC * hid, width), BF16),
            pltpu.SemaphoreType.DMA((NC,)),
        ],
        compiler_params=SMALL,
        name="down",
    )(place, *blocks, *weights)


def sum_y_kernel(parts, out):
    total = parts[0].astype(F32)
    for n in range(1, NY):
        total = total + parts[n].astype(F32)

    def source(i):
        return (
            (lax.shift_right_logical(i, 1) & 3) * 16 + lax.shift_right_logical(i, 3) * 2 + (i & 1)
        )

    out[...] = dot(moved(out.shape[0], source), total.astype(BF16)).astype(BF16)


def sum_y(parts):
    return pl.pallas_call(
        sum_y_kernel,
        out_shape=jax.ShapeDtypeStruct(parts.shape[1:], BF16),
        in_specs=[VMEM],
        out_specs=VMEM,
        compiler_params=SMALL,
        name="sum_y",
    )(parts)


def on_device(
    queries, new_entries, cache, lengths, hidden, w_uv, w_o, ffn_gain, w_gate, w_up, w_down
):
    y, z, c, x = (lax.axis_index(a) for a in ("y", "z", "c", "x"))
    place = jnp.stack([y, z, c, x]).astype(jnp.int32)
    rolls, steps = queries.shape[:2]
    pair = NC * w_o.shape[1]
    width, hid = w_gate.shape
    cache = cache.transpose(0, 2, 1)
    hidden = hidden.transpose(1, 2, 0).reshape(-1, hidden.shape[0])
    w_o, w_gate, w_up = w_o.T, w_gate.T, w_up.T

    def other(v):
        return lax.ppermute(v, "c", shift(NC, 1))

    with jax.named_scope("attend"):
        depth = w_o.shape[1] // NY
        w_o = lax.all_to_all(cut(w_o, NY), "y", 0, 0)
        swapped = [other(v) for v in (hidden, w_gate, w_up, w_down)]
        head_out = attend(queries, new_entries, cache, lengths, w_uv)
        head_out, w_o, swapped = lax.optimization_barrier((head_out, w_o, swapped))
        hidden_alien, w_gate_alien, w_up_alien, w_down_alien = swapped

    with jax.named_scope("gather_heads"):
        w_o_alien = other(w_o)
        added = stream(place, hidden, hidden_alien, steps)
        near = lax.all_to_all(head_out.reshape(NY * NZ, -1, depth), ("y", "z"), 0, 0)
        near, w_o_alien, added = lax.optimization_barrier((near, w_o_alien, added))

    with jax.named_scope("project"):
        parts = project(place, near.reshape(-1, depth), (w_o, w_o_alien), added)

    with jax.named_scope("sum_heads"):
        parts = lax.all_to_all(parts, ("y", "x"), 0, 0)
        resid = sum_heads(parts)

    with jax.named_scope("gather_resid"):
        resid = lax.all_to_all(resid, "z", 0, 0)
        resid = lax.all_gather(resid, "y")

    with jax.named_scope("gate_up"):
        gain = lax.dynamic_slice_in_dim(ffn_gain, x * width, width, 0).astype(F32)
        messages = gate_up(
            place, gain.reshape(NZ, pair), resid, (w_gate, w_up, w_gate_alien, w_up_alien)
        )

    with jax.named_scope("sum_gate_up"):
        messages = [messages[0]] + [
            lax.ppermute(messages[k], "x", shift(NX, k)) for k in range(1, NX)
        ]
        act = activate(messages, NX * width, hid)

    with jax.named_scope("down"):
        out = down(place, fetch(act, "x", NX), (w_down, w_down_alien))

    with jax.named_scope("sum_y"):
        out = lax.all_to_all(out.reshape(NY, -1, width), "y", 0, 0)
        out = sum_y(out)

    with jax.named_scope("sum_z"):
        out = lax.all_to_all(out.reshape(NZ, rolls * steps, width), "z", 0, 0)
        out = jnp.sum(out.astype(F32), axis=0)

    with jax.named_scope("finish"):
        own = lax.dynamic_slice_in_dim(resid, (y * NZ + z) * steps, steps, 2)
        own = own.transpose(0, 2, 1, 3).reshape(rolls * steps, width)
        out = (own.astype(F32) + out).astype(BF16)
    return out.reshape(rolls, steps, width)


def solution(mesh):
    fine = Mesh(mesh.devices.reshape(NY, NZ, NC, NX), ("y", "z", "c", "x"))
    dp = ("y", "z", "c")
    placed = (
        P(dp, None, "x", None),
        P(dp, None, None),
        P(dp, None, None),
        P(dp),
        P(None, None, dp),
        P("x", None, None),
        P("x", dp),
        P(),
        P("x", dp),
        P("x", dp),
        P(dp, "x"),
    )
    return jax.shard_map(
        on_device, mesh=fine, in_specs=placed, out_specs=P(dp, None, "x"), check_vma=False
    )
```

```python
import jax
import jax.numpy as jnp
from jax import lax
from jax.experimental import pallas as pl
from jax.experimental.pallas import tpu as pltpu
from jax.sharding import Mesh
from jax.sharding import PartitionSpec as P

ROPE = 64
NOPE = 128
NY, NZ, NC, NX = 4, 8, 2, 4
F32 = jnp.float32
BF16 = jnp.bfloat16
VMEM = pl.BlockSpec(memory_space=pltpu.VMEM)
ANY = pl.BlockSpec(memory_space=pl.ANY)
HBM = pl.BlockSpec(memory_space=pltpu.HBM)
SMEM = pl.BlockSpec(memory_space=pltpu.SMEM)
LARGE = pltpu.CompilerParams(vmem_limit_bytes=52 * 1024 * 1024)
ATT = pltpu.CompilerParams(vmem_limit_bytes=60 * 1024 * 1024)
CUT = pltpu.CompilerParams(vmem_limit_bytes=60 * 1024 * 1024)
MIDDLE = pltpu.CompilerParams(vmem_limit_bytes=44 * 1024 * 1024)
SMALL = pltpu.CompilerParams(vmem_limit_bytes=16 * 1024 * 1024)


def dot(a, b):
    return jnp.dot(a, b, preferred_element_type=F32)


def dot_t(a, b):
    return lax.dot_general(a, b, (((1,), (1,)), ((), ())), preferred_element_type=F32)


def shift(n, k):
    return [(i, (i + k) % n) for i in range(n)]


def fetch(v, axis, n):
    return [v] + [lax.ppermute(v, axis, shift(n, -k)) for k in range(1, n)]


def moved(rows, source):
    i = lax.broadcasted_iota(jnp.int32, (rows, rows), 0)
    j = lax.broadcasted_iota(jnp.int32, (rows, rows), 1)
    return (source(i) == j).astype(BF16)


def attend_kernel(
    scale, lengths, q, new_entries, entries, w_uv, out, queries, latents, cache, w, sems
):
    count, entry, span = cache.shape
    steps, heads = queries.shape[1:3]
    latent = latents.shape[2]
    value = w.shape[2]
    loads = [pltpu.make_async_copy(entries.at[r], cache.at[r], sems.at[r]) for r in range(count)]
    loads.append(pltpu.make_async_copy(w_uv, w, sems.at[count]))
    first = pltpu.make_async_copy(q, queries, sems.at[count + 1])
    first.start()
    for load in loads:
        load.start()
    first.wait()
    for r in range(count):
        rows = queries[r].reshape(steps * heads, entry)
        fresh = new_entries[r].astype(F32)
        step = lax.broadcasted_iota(jnp.int32, (steps * heads, 1), 0) // heads
        late = []
        for n in range(steps):
            s = jnp.sum(rows.astype(F32) * fresh[n : n + 1, :], axis=1, keepdims=True) * scale
            late.append(jnp.where(step >= n, s, -1e30))
        loads[r].wait()
        scores = dot(rows, cache[r]) * scale
        valid = lax.broadcasted_iota(jnp.int32, scores.shape, 1) < lengths[r]
        scores = jnp.where(valid, scores, -1e30)
        top = jnp.max(scores, axis=1, keepdims=True)
        for s in late:
            top = jnp.maximum(top, s)
        weights = jnp.exp(scores - top)
        late = [jnp.exp(s - top) for s in late]
        share = 1.0 / (jnp.sum(weights, axis=1, keepdims=True) + sum(late))
        result = dot_t((weights * share).astype(BF16), cache[r, :latent, :])
        for n in range(steps):
            result = result + (late[n] * share).astype(BF16).astype(F32) * fresh[n : n + 1, :latent]
        result = result.astype(BF16).astype(F32)
        for t in range(steps):
            latents[:, r * steps + t, :] = result[t * heads : (t + 1) * heads]
    loads[count].wait()
    for h in range(heads):
        part, n = divmod(h, heads // NY)
        result = dot(latents[h].astype(BF16), w[h]).astype(BF16)
        for b in range(NZ):
            out[part, b, :, n * value : (n + 1) * value] = result


def attend(queries, new_entries, cache, lengths, w_uv):
    rolls, steps, heads, entry = queries.shape
    _, latent, value = w_uv.shape
    return pl.pallas_call(
        lambda *refs: attend_kernel((NOPE + ROPE) ** (-0.5), *refs),
        out_shape=jax.ShapeDtypeStruct((NY, NZ, rolls * steps, heads * value // NY), BF16),
        in_specs=[SMEM, HBM, VMEM, HBM, HBM],
        out_specs=VMEM,
        scratch_shapes=[
            pltpu.VMEM(queries.shape, BF16),
            pltpu.VMEM((heads, rolls * steps, latent), F32),
            pltpu.VMEM(cache.shape, BF16),
            pltpu.VMEM(w_uv.shape, BF16),
            pltpu.SemaphoreType.DMA((rolls + 2,)),
        ],
        compiler_params=ATT,
        name="attend",
    )(lengths, queries, new_entries, cache, w_uv)


def cut_kernel(v, out, sems):
    blocks, _, depth = out.shape
    moves = [
        pltpu.make_async_copy(v.at[:, b * depth : (b + 1) * depth], out.at[b], sems.at[b])
        for b in range(blocks)
    ]
    for move in moves:
        move.start()
    for move in moves:
        move.wait()


def cut(v, blocks):
    rows, width = v.shape
    return pl.pallas_call(
        cut_kernel,
        out_shape=jax.ShapeDtypeStruct((blocks, rows, width // blocks), v.dtype),
        in_specs=[HBM],
        out_specs=VMEM,
        scratch_shapes=[pltpu.SemaphoreType.DMA((blocks,))],
        compiler_params=CUT,
        name="cut",
    )(v)


def stream_kernel(steps, place, hidden, hidden_alien, out):
    c, x = place[2], place[3]
    size = out.shape[0]

    def chosen(values):
        cols = values.shape[0] // steps
        i = lax.broadcasted_iota(jnp.int32, (size, values.shape[1]), 0)
        j = lax.broadcasted_iota(jnp.int32, (size, values.shape[1]), 1)
        here = (lax.shift_right_logical(i, 1) * NC + c) * NX + x == j
        total = 0.0
        for t in range(steps):
            rows = (here & ((i & 1) == t)).astype(BF16)
            total = total + dot_t(rows, values[t * cols : (t + 1) * cols])
        return total

    own, alien = chosen(hidden), chosen(hidden_alien)
    out[...] = jnp.concatenate(
        [jnp.where(c == 0, own, alien), jnp.where(c == 0, alien, own)], axis=1
    ).astype(BF16)


def stream(place, hidden, hidden_alien, steps):
    rows = NY * NZ * steps
    return pl.pallas_call(
        lambda *refs: stream_kernel(steps, *refs),
        out_shape=jax.ShapeDtypeStruct((rows, NC * hidden.shape[0] // steps), BF16),
        in_specs=[SMEM, VMEM, VMEM],
        out_specs=VMEM,
        compiler_params=SMALL,
        name="stream",
    )(place, hidden, hidden_alien)


def project_kernel(place, lhs_in, w_own, w_alien, added, out, lhs, w, sems):
    y, z, c, x = place[0], place[1], place[2], place[3]
    blocks, cols = w_own.shape[:2]
    loads = [pltpu.make_async_copy(lhs_in, lhs, sems.at[0])]
    for n, (v, at) in enumerate(((w_own, c), (w_alien, 1 - c))):
        for b in range(blocks):
            to = pl.multiple_of((b * NC + at) * cols, 16)
            loads.append(
                pltpu.make_async_copy(v.at[b], w.at[pl.ds(to, cols)], sems.at[1 + n * blocks + b])
            )
    for load in loads:
        load.start()
    rows, size = lhs.shape[0], out.shape[1]

    def source(i):
        roll = lax.shift_right_logical(i, 6)
        zz = lax.shift_right_logical(i, 1) & 7
        yy = lax.shift_right_logical(i, 4) & 3
        return yy * 64 + zz * 8 + roll * 2 + (i & 1)

    order = moved(rows, source)
    for load in loads:
        load.wait()
    pair = NC * cols
    for b in range(blocks):
        part = dot_t(lhs[...], w[b * pair : (b + 1) * pair]).astype(BF16)
        part = dot(order, part)
        for j in range(NX):
            piece = part[j * size : (j + 1) * size]
            piece = piece + jnp.where((j == x) & (b == y), added[...].astype(F32), 0.0)
            out[j * blocks + b] = piece.astype(BF16)


def project(place, lhs, weights, added):
    rows, depth = lhs.shape
    blocks, cols, _ = weights[0].shape
    return pl.pallas_call(
        project_kernel,
        out_shape=jax.ShapeDtypeStruct((NX * blocks, rows // NX, NC * cols), BF16),
        in_specs=[SMEM, ANY] + [HBM] * NC + [VMEM],
        out_specs=VMEM,
        scratch_shapes=[
            pltpu.VMEM((rows, depth), BF16),
            pltpu.VMEM((blocks * NC * cols, depth), BF16),
            pltpu.SemaphoreType.DMA((1 + NC * blocks,)),
        ],
        compiler_params=SMALL,
        name="project",
    )(place, lhs, *weights, added)


def sum_heads_kernel(parts, out):
    total = parts[0].astype(F32)
    for n in range(1, parts.shape[0]):
        total = total + parts[n].astype(F32)
    for b in range(out.shape[0]):
        out[b] = total.astype(BF16)


def sum_heads(parts):
    return pl.pallas_call(
        sum_heads_kernel,
        out_shape=jax.ShapeDtypeStruct((NZ,) + parts.shape[1:], BF16),
        in_specs=[VMEM],
        out_specs=VMEM,
        compiler_params=SMALL,
        name="sum_heads",
    )(parts)


def stacked_kernel(count, *refs):
    parts, out, sems = refs[:count], refs[count], refs[count + 1]
    rows = parts[0].shape[0]
    loads = [
        pltpu.make_async_copy(v, out.at[pl.ds(n * rows, rows)], sems.at[n])
        for n, v in enumerate(parts)
    ]
    for load in loads:
        load.start()
    for load in loads:
        load.wait()


def stacked(parts):
    rows, width = parts[0].shape
    return pl.pallas_call(
        lambda *refs: stacked_kernel(len(parts), *refs),
        out_shape=jax.ShapeDtypeStruct((len(parts) * rows, width), parts[0].dtype),
        in_specs=[HBM] * len(parts),
        out_specs=VMEM,
        scratch_shapes=[pltpu.SemaphoreType.DMA((len(parts),))],
        compiler_params=MIDDLE,
        name="stacked",
    )(*parts)


def gate_up_kernel(place, gain, b0, b1, b2, b3, w, o0, o1, o2, o3, blocks, scaled, sems):
    hid = w.shape[0] // 4
    y, x = place[0], place[3]
    loads = [
        pltpu.make_async_copy(v, blocks.at[(y + n) & 3], sems.at[n])
        for n, v in enumerate((b0, b1, b2, b3))
    ]
    for load in loads:
        load.start()
    ny, nz, rows, cols = blocks.shape
    for load in loads:
        load.wait()
    squares = [0.0] * ny
    for b in range(nz):
        for k in range(ny):
            block = blocks[(x + k) & 3, b].astype(F32)
            squares[k] = squares[k] + jnp.sum(block * block, axis=1, keepdims=True)
            scaled[k * rows : (k + 1) * rows, b * cols : (b + 1) * cols] = (
                block * gain[b : b + 1, :]
            ).astype(BF16)
    total = dot_t(scaled[...], w[...]).astype(BF16)
    for k, out in enumerate((o0, o1, o2, o3)):
        out[:, : 4 * hid] = total[k * rows : (k + 1) * rows]
        out[:, 4 * hid :] = jnp.broadcast_to(squares[k].astype(BF16), (rows, 128))


def gate_up(place, gain, blocks, w):
    ny, (nz, rows, cols) = len(blocks), blocks[0].shape
    units, width = w.shape
    return pl.pallas_call(
        gate_up_kernel,
        out_shape=[jax.ShapeDtypeStruct((rows, units + 128), BF16)] * ny,
        in_specs=[SMEM, VMEM] + [ANY] * ny + [VMEM],
        out_specs=[VMEM] * ny,
        scratch_shapes=[
            pltpu.VMEM((ny,) + blocks[0].shape, BF16),
            pltpu.VMEM((ny * rows, width), BF16),
            pltpu.SemaphoreType.DMA((ny,)),
        ],
        compiler_params=SMALL,
        name="gate_up",
    )(place, gain, *blocks, w)


def activate_kernel(features, hid, m0, m1, m2, m3, act):
    both = (m0[...].astype(F32) + m1[...].astype(F32)) + (
        m2[...].astype(F32) + m3[...].astype(F32)
    )
    both = both[:, : 4 * hid] * lax.rsqrt(both[:, 4 * hid : 4 * hid + 1] / features + 1e-06)
    for n in range(NC):
        gate = both[:, 2 * n * hid : (2 * n + 1) * hid]
        up = both[:, (2 * n + 1) * hid : (2 * n + 2) * hid]
        act[:, n * hid : (n + 1) * hid] = (jax.nn.silu(gate) * up).astype(BF16)


def activate(messages, features, hid):
    return pl.pallas_call(
        lambda *refs: activate_kernel(features, hid, *refs),
        out_shape=jax.ShapeDtypeStruct((messages[0].shape[0], NC * hid), BF16),
        in_specs=[VMEM] * NX,
        out_specs=VMEM,
        compiler_params=SMALL,
        name="activate",
    )(*messages)


def down_kernel(place, a0, a1, a2, a3, w_own, w_alien, out, act, w, sems):
    hid = w_own.shape[0]
    loads = [
        pltpu.make_async_copy(v, w.at[pl.ds(n * hid, hid)], sems.at[n])
        for n, v in enumerate((w_own, w_alien))
    ]
    for load in loads:
        load.start()
    x = place[3]
    rows = a0.shape[0]
    for n, a in enumerate((a0, a1, a2, a3)):
        act[n * rows : (n + 1) * rows] = a[...]
    for load in loads:
        load.wait()
    total = dot(act[...], w[...]).astype(BF16)
    part = rows // NY
    for n in range(NX):
        for b in range(NY):
            start = n * rows + b * part
            out[b, (x + n) & 3] = total[start : start + part]


def down(place, blocks, weights):
    rows = blocks[0].shape[0]
    hid, width = weights[0].shape
    return pl.pallas_call(
        down_kernel,
        out_shape=jax.ShapeDtypeStruct((NY, NX, rows // NY, width), BF16),
        in_specs=[SMEM] + [VMEM] * NX + [HBM] * NC,
        out_specs=VMEM,
        scratch_shapes=[
            pltpu.VMEM((NX * rows, NC * hid), BF16),
            pltpu.VMEM((NC * hid, width), BF16),
            pltpu.SemaphoreType.DMA((NC,)),
        ],
        compiler_params=SMALL,
        name="down",
    )(place, *blocks, *weights)


def sum_y_kernel(parts, out):
    total = parts[0].astype(F32)
    for n in range(1, NY):
        total = total + parts[n].astype(F32)

    def source(i):
        return (
            (lax.shift_right_logical(i, 1) & 3) * 16 + lax.shift_right_logical(i, 3) * 2 + (i & 1)
        )

    out[...] = dot(moved(out.shape[0], source), total.astype(BF16)).astype(BF16)


def sum_y(parts):
    return pl.pallas_call(
        sum_y_kernel,
        out_shape=jax.ShapeDtypeStruct(parts.shape[1:], BF16),
        in_specs=[VMEM],
        out_specs=VMEM,
        compiler_params=SMALL,
        name="sum_y",
    )(parts)


def on_device(
    queries, new_entries, cache, lengths, hidden, w_uv, w_o, ffn_gain, w_gate, w_up, w_down
):
    y, z, c, x = (lax.axis_index(a) for a in ("y", "z", "c", "x"))
    place = jnp.stack([y, z, c, x]).astype(jnp.int32)
    rolls, steps = queries.shape[:2]
    pair = NC * w_o.shape[1]
    width, hid = w_gate.shape
    cache = cache.transpose(0, 2, 1)
    hidden = hidden.transpose(1, 2, 0).reshape(-1, hidden.shape[0])
    w_o, w_gate, w_up = w_o.T, w_gate.T, w_up.T

    def other(v):
        return lax.ppermute(v, "c", shift(NC, 1))

    with jax.named_scope("attend"):
        depth = w_o.shape[1] // NY
        w_o = lax.all_to_all(cut(w_o, NY), "y", 0, 0)
        swapped = [other(v) for v in (hidden, w_gate, w_up, w_down)]
        head_out = attend(queries, new_entries, cache, lengths, w_uv)
        head_out, w_o, swapped = lax.optimization_barrier((head_out, w_o, swapped))
        hidden_alien, w_gate_alien, w_up_alien, w_down_alien = swapped

    with jax.named_scope("gather_heads"):
        w_o_alien = other(w_o)
        added = stream(place, hidden, hidden_alien, steps)
        near = lax.all_to_all(head_out.reshape(NY * NZ, -1, depth), ("y", "z"), 0, 0)
        near, w_o_alien, added = lax.optimization_barrier((near, w_o_alien, added))

    with jax.named_scope("project"):
        parts = project(place, near.reshape(-1, depth), (w_o, w_o_alien), added)

    with jax.named_scope("sum_heads"):
        parts = lax.all_to_all(parts, ("y", "x"), 0, 0)
        resid = sum_heads(parts)

    with jax.named_scope("gather_resid"):
        resid = lax.all_to_all(resid, "z", 0, 0)
        resid, ready = lax.optimization_barrier(
            (resid, (w_gate, w_up, w_gate_alien, w_up_alien))
        )
        blocks = fetch(resid, "y", NY)
        weights = stacked(ready)

    with jax.named_scope("gate_up"):
        gain = lax.dynamic_slice_in_dim(ffn_gain, x * width, width, 0).astype(F32)
        messages = gate_up(place, gain.reshape(NZ, pair), blocks, weights)

    with jax.named_scope("sum_gate_up"):
        messages = [messages[0]] + [
            lax.ppermute(messages[k], "x", shift(NX, k)) for k in range(1, NX)
        ]
        act = activate(messages, NX * width, hid)

    with jax.named_scope("down"):
        out = down(place, fetch(act, "x", NX), (w_down, w_down_alien))

    with jax.named_scope("sum_y"):
        out = lax.all_to_all(out.reshape(NY, -1, width), "y", 0, 0)
        out = sum_y(out)

    with jax.named_scope("sum_z"):
        out = lax.all_to_all(out.reshape(NZ, rolls * steps, width), "z", 0, 0)
        out = jnp.sum(out.astype(F32), axis=0)

    with jax.named_scope("finish"):
        at = (y * NZ + z) * steps
        own = jnp.stack([lax.dynamic_slice_in_dim(b, at, steps, 1) for b in blocks])
        own = jnp.concatenate([own, own], axis=0)
        own = lax.dynamic_slice_in_dim(own, lax.rem(NY - y, NY), NY, 0)
        own = own.transpose(0, 2, 1, 3).reshape(rolls * steps, width)
        out = (own.astype(F32) + out).astype(BF16)
    return out.reshape(rolls, steps, width)


def solution(mesh):
    fine = Mesh(mesh.devices.reshape(NY, NZ, NC, NX), ("y", "z", "c", "x"))
    dp = ("y", "z", "c")
    placed = (
        P(dp, None, "x", None),
        P(dp, None, None),
        P(dp, None, None),
        P(dp),
        P(None, None, dp),
        P("x", None, None),
        P("x", dp),
        P(),
        P("x", dp),
        P("x", dp),
        P(dp, "x"),
    )
    return jax.shard_map(
        on_device, mesh=fine, in_specs=placed, out_specs=P(dp, None, "x"), check_vma=False
    )
```

```python
import jax
import jax.numpy as jnp
from jax import lax
from jax.experimental import pallas as pl
from jax.experimental.pallas import tpu as pltpu
from jax.sharding import Mesh
from jax.sharding import PartitionSpec as P

ROPE = 64
NOPE = 128
NY, NZ, NC, NX = 4, 8, 2, 4
F32 = jnp.float32
BF16 = jnp.bfloat16
VMEM = pl.BlockSpec(memory_space=pltpu.VMEM)
ANY = pl.BlockSpec(memory_space=pl.ANY)
HBM = pl.BlockSpec(memory_space=pltpu.HBM)
SMEM = pl.BlockSpec(memory_space=pltpu.SMEM)
LARGE = pltpu.CompilerParams(vmem_limit_bytes=52 * 1024 * 1024)
ATT = pltpu.CompilerParams(vmem_limit_bytes=60 * 1024 * 1024)
CUT = pltpu.CompilerParams(vmem_limit_bytes=60 * 1024 * 1024)
MIDDLE = pltpu.CompilerParams(vmem_limit_bytes=44 * 1024 * 1024)
SMALL = pltpu.CompilerParams(vmem_limit_bytes=16 * 1024 * 1024)


def dot(a, b):
    return jnp.dot(a, b, preferred_element_type=F32)


def dot_t(a, b):
    return lax.dot_general(a, b, (((1,), (1,)), ((), ())), preferred_element_type=F32)


def shift(n, k):
    return [(i, (i + k) % n) for i in range(n)]


def fetch(v, axis, n):
    return [v] + [lax.ppermute(v, axis, shift(n, -k)) for k in range(1, n)]


def moved(rows, source):
    i = lax.broadcasted_iota(jnp.int32, (rows, rows), 0)
    j = lax.broadcasted_iota(jnp.int32, (rows, rows), 1)
    return (source(i) == j).astype(BF16)


def attend_kernel(
    scale, lengths, q, new_entries, entries, w_uv, out, queries, latents, cache, w, sems
):
    count, entry, span = cache.shape
    steps, heads = queries.shape[1:3]
    latent = latents.shape[2]
    value = w.shape[2]
    loads = [pltpu.make_async_copy(entries.at[r], cache.at[r], sems.at[r]) for r in range(count)]
    loads.append(pltpu.make_async_copy(w_uv, w, sems.at[count]))
    first = pltpu.make_async_copy(q, queries, sems.at[count + 1])
    first.start()
    for load in loads:
        load.start()
    first.wait()
    for r in range(count):
        rows = queries[r].reshape(steps * heads, entry)
        fresh = new_entries[r].astype(F32)
        step = lax.broadcasted_iota(jnp.int32, (steps * heads, 1), 0) // heads
        late = []
        for n in range(steps):
            s = jnp.sum(rows.astype(F32) * fresh[n : n + 1, :], axis=1, keepdims=True) * scale
            late.append(jnp.where(step >= n, s, -1e30))
        loads[r].wait()
        scores = dot(rows, cache[r]) * scale
        valid = lax.broadcasted_iota(jnp.int32, scores.shape, 1) < lengths[r]
        scores = jnp.where(valid, scores, -1e30)
        top = jnp.max(scores, axis=1, keepdims=True)
        for s in late:
            top = jnp.maximum(top, s)
        weights = jnp.exp(scores - top)
        late = [jnp.exp(s - top) for s in late]
        share = 1.0 / (jnp.sum(weights, axis=1, keepdims=True) + sum(late))
        result = dot_t((weights * share).astype(BF16), cache[r, :latent, :])
        for n in range(steps):
            result = result + (late[n] * share).astype(BF16).astype(F32) * fresh[n : n + 1, :latent]
        result = result.astype(BF16).astype(F32)
        for t in range(steps):
            latents[:, r * steps + t, :] = result[t * heads : (t + 1) * heads]
    loads[count].wait()
    for h in range(heads):
        part, n = divmod(h, heads // NY)
        result = dot(latents[h].astype(BF16), w[h]).astype(BF16)
        for b in range(NZ):
            out[part, b, :, n * value : (n + 1) * value] = result


def attend(queries, new_entries, cache, lengths, w_uv):
    rolls, steps, heads, entry = queries.shape
    _, latent, value = w_uv.shape
    return pl.pallas_call(
        lambda *refs: attend_kernel((NOPE + ROPE) ** (-0.5), *refs),
        out_shape=jax.ShapeDtypeStruct((NY, NZ, rolls * steps, heads * value // NY), BF16),
        in_specs=[SMEM, HBM, VMEM, HBM, HBM],
        out_specs=VMEM,
        scratch_shapes=[
            pltpu.VMEM(queries.shape, BF16),
            pltpu.VMEM((heads, rolls * steps, latent), F32),
            pltpu.VMEM(cache.shape, BF16),
            pltpu.VMEM(w_uv.shape, BF16),
            pltpu.SemaphoreType.DMA((rolls + 2,)),
        ],
        compiler_params=ATT,
        name="attend",
    )(lengths, queries, new_entries, cache, w_uv)


def cut_kernel(v, out, sems):
    blocks, _, depth = out.shape
    moves = [
        pltpu.make_async_copy(v.at[:, b * depth : (b + 1) * depth], out.at[b], sems.at[b])
        for b in range(blocks)
    ]
    for move in moves:
        move.start()
    for move in moves:
        move.wait()


def cut(v, blocks):
    rows, width = v.shape
    return pl.pallas_call(
        cut_kernel,
        out_shape=jax.ShapeDtypeStruct((blocks, rows, width // blocks), v.dtype),
        in_specs=[HBM],
        out_specs=VMEM,
        scratch_shapes=[pltpu.SemaphoreType.DMA((blocks,))],
        compiler_params=CUT,
        name="cut",
    )(v)


def stream_kernel(steps, place, hidden, hidden_alien, out):
    c, x = place[2], place[3]
    size = out.shape[0]

    def chosen(values):
        cols = values.shape[0] // steps
        i = lax.broadcasted_iota(jnp.int32, (size, values.shape[1]), 0)
        j = lax.broadcasted_iota(jnp.int32, (size, values.shape[1]), 1)
        here = (lax.shift_right_logical(i, 1) * NC + c) * NX + x == j
        total = 0.0
        for t in range(steps):
            rows = (here & ((i & 1) == t)).astype(BF16)
            total = total + dot_t(rows, values[t * cols : (t + 1) * cols])
        return total

    own, alien = chosen(hidden), chosen(hidden_alien)
    out[...] = jnp.concatenate(
        [jnp.where(c == 0, own, alien), jnp.where(c == 0, alien, own)], axis=1
    ).astype(BF16)


def stream(place, hidden, hidden_alien, steps):
    rows = NY * NZ * steps
    return pl.pallas_call(
        lambda *refs: stream_kernel(steps, *refs),
        out_shape=jax.ShapeDtypeStruct((rows, NC * hidden.shape[0] // steps), BF16),
        in_specs=[SMEM, VMEM, VMEM],
        out_specs=VMEM,
        compiler_params=SMALL,
        name="stream",
    )(place, hidden, hidden_alien)


def project_kernel(place, lhs_in, w_own, w_alien, added, out, lhs, w, sems):
    y, z, c, x = place[0], place[1], place[2], place[3]
    blocks, cols = w_own.shape[:2]
    loads = [pltpu.make_async_copy(lhs_in, lhs, sems.at[0])]
    for n, (v, at) in enumerate(((w_own, c), (w_alien, 1 - c))):
        for b in range(blocks):
            to = pl.multiple_of((b * NC + at) * cols, 16)
            loads.append(
                pltpu.make_async_copy(v.at[b], w.at[pl.ds(to, cols)], sems.at[1 + n * blocks + b])
            )
    for load in loads:
        load.start()
    rows, size = lhs.shape[0], out.shape[1]

    def source(i):
        roll = lax.shift_right_logical(i, 6)
        zz = lax.shift_right_logical(i, 1) & 7
        yy = lax.shift_right_logical(i, 4) & 3
        return yy * 64 + zz * 8 + roll * 2 + (i & 1)

    order = moved(rows, source)
    for load in loads:
        load.wait()
    pair = NC * cols
    for b in range(blocks):
        part = dot_t(lhs[...], w[b * pair : (b + 1) * pair]).astype(BF16)
        part = dot(order, part)
        for j in range(NX):
            piece = part[j * size : (j + 1) * size]
            piece = piece + jnp.where((j == x) & (b == y), added[...].astype(F32), 0.0)
            out[j * blocks + b] = piece.astype(BF16)


def project(place, lhs, weights, added):
    rows, depth = lhs.shape
    blocks, cols, _ = weights[0].shape
    return pl.pallas_call(
        project_kernel,
        out_shape=jax.ShapeDtypeStruct((NX * blocks, rows // NX, NC * cols), BF16),
        in_specs=[SMEM, ANY] + [HBM] * NC + [VMEM],
        out_specs=VMEM,
        scratch_shapes=[
            pltpu.VMEM((rows, depth), BF16),
            pltpu.VMEM((blocks * NC * cols, depth), BF16),
            pltpu.SemaphoreType.DMA((1 + NC * blocks,)),
        ],
        compiler_params=SMALL,
        name="project",
    )(place, lhs, *weights, added)


def sum_heads_kernel(parts, out):
    total = parts[0].astype(F32)
    for n in range(1, parts.shape[0]):
        total = total + parts[n].astype(F32)
    for b in range(out.shape[0]):
        out[b] = total.astype(BF16)


def sum_heads(parts):
    return pl.pallas_call(
        sum_heads_kernel,
        out_shape=jax.ShapeDtypeStruct((NZ,) + parts.shape[1:], BF16),
        in_specs=[VMEM],
        out_specs=VMEM,
        compiler_params=SMALL,
        name="sum_heads",
    )(parts)


def stacked_kernel(count, *refs):
    parts, out, sems = refs[:count], refs[count], refs[count + 1]
    rows = parts[0].shape[0]
    loads = [
        pltpu.make_async_copy(v, out.at[pl.ds(n * rows, rows)], sems.at[n])
        for n, v in enumerate(parts)
    ]
    for load in loads:
        load.start()
    for load in loads:
        load.wait()


def stacked(parts):
    rows, width = parts[0].shape
    return pl.pallas_call(
        lambda *refs: stacked_kernel(len(parts), *refs),
        out_shape=jax.ShapeDtypeStruct((len(parts) * rows, width), parts[0].dtype),
        in_specs=[HBM] * len(parts),
        out_specs=VMEM,
        scratch_shapes=[pltpu.SemaphoreType.DMA((len(parts),))],
        compiler_params=MIDDLE,
        name="stacked",
    )(*parts)


def gate_up_kernel(place, gain, b0, b1, b2, b3, w, o0, o1, o2, o3, blocks, scaled, sems):
    hid = w.shape[0] // 4
    y, x = place[0], place[3]
    loads = [
        pltpu.make_async_copy(v, blocks.at[(y + n) & 3], sems.at[n])
        for n, v in enumerate((b0, b1, b2, b3))
    ]
    for load in loads:
        load.start()
    ny, nz, rows, cols = blocks.shape
    for load in loads:
        load.wait()
    squares = [0.0] * ny
    for b in range(nz):
        for k in range(ny):
            block = blocks[(x + k) & 3, b].astype(F32)
            squares[k] = squares[k] + jnp.sum(block * block, axis=1, keepdims=True)
            scaled[k * rows : (k + 1) * rows, b * cols : (b + 1) * cols] = (
                block * gain[b : b + 1, :]
            ).astype(BF16)
    total = dot_t(scaled[...], w[...]).astype(BF16)
    for k, out in enumerate((o0, o1, o2, o3)):
        out[:, : 4 * hid] = total[k * rows : (k + 1) * rows]
        out[:, 4 * hid :] = jnp.broadcast_to(squares[k].astype(BF16), (rows, 128))


def gate_up(place, gain, blocks, w):
    ny, (nz, rows, cols) = len(blocks), blocks[0].shape
    units, width = w.shape
    return pl.pallas_call(
        gate_up_kernel,
        out_shape=[jax.ShapeDtypeStruct((rows, units + 128), BF16)] * ny,
        in_specs=[SMEM, VMEM] + [ANY] * ny + [VMEM],
        out_specs=[VMEM] * ny,
        scratch_shapes=[
            pltpu.VMEM((ny,) + blocks[0].shape, BF16),
            pltpu.VMEM((ny * rows, width), BF16),
            pltpu.SemaphoreType.DMA((ny,)),
        ],
        compiler_params=SMALL,
        name="gate_up",
    )(place, gain, *blocks, w)


def activate_kernel(features, hid, m0, m1, m2, m3, act):
    both = (m0[...].astype(F32) + m1[...].astype(F32)) + (
        m2[...].astype(F32) + m3[...].astype(F32)
    )
    both = both[:, : 4 * hid] * lax.rsqrt(both[:, 4 * hid : 4 * hid + 1] / features + 1e-06)
    for n in range(NC):
        gate = both[:, 2 * n * hid : (2 * n + 1) * hid]
        up = both[:, (2 * n + 1) * hid : (2 * n + 2) * hid]
        act[:, n * hid : (n + 1) * hid] = (jax.nn.silu(gate) * up).astype(BF16)


def activate(messages, features, hid):
    return pl.pallas_call(
        lambda *refs: activate_kernel(features, hid, *refs),
        out_shape=jax.ShapeDtypeStruct((messages[0].shape[0], NC * hid), BF16),
        in_specs=[VMEM] * NX,
        out_specs=VMEM,
        compiler_params=SMALL,
        name="activate",
    )(*messages)


def down_kernel(place, a0, a1, a2, a3, w, out, act):
    x = place[3]
    rows = a0.shape[0]
    for n, a in enumerate((a0, a1, a2, a3)):
        act[n * rows : (n + 1) * rows] = a[...]
    total = dot(act[...], w[...]).astype(BF16)
    part = rows // NY
    for n in range(NX):
        for b in range(NY):
            start = n * rows + b * part
            out[b, (x + n) & 3] = total[start : start + part]


def down(place, blocks, w):
    rows = blocks[0].shape[0]
    units, width = w.shape
    return pl.pallas_call(
        down_kernel,
        out_shape=jax.ShapeDtypeStruct((NY, NX, rows // NY, width), BF16),
        in_specs=[SMEM] + [VMEM] * (NX + 1),
        out_specs=VMEM,
        scratch_shapes=[
            pltpu.VMEM((NX * rows, units), BF16),
        ],
        compiler_params=SMALL,
        name="down",
    )(place, *blocks, w)


def sum_y_kernel(parts, out):
    total = parts[0].astype(F32)
    for n in range(1, NY):
        total = total + parts[n].astype(F32)

    def source(i):
        return (
            (lax.shift_right_logical(i, 1) & 3) * 16 + lax.shift_right_logical(i, 3) * 2 + (i & 1)
        )

    out[...] = dot(moved(out.shape[0], source), total.astype(BF16)).astype(BF16)


def sum_y(parts):
    return pl.pallas_call(
        sum_y_kernel,
        out_shape=jax.ShapeDtypeStruct(parts.shape[1:], BF16),
        in_specs=[VMEM],
        out_specs=VMEM,
        compiler_params=SMALL,
        name="sum_y",
    )(parts)


def on_device(
    queries, new_entries, cache, lengths, hidden, w_uv, w_o, ffn_gain, w_gate, w_up, w_down
):
    y, z, c, x = (lax.axis_index(a) for a in ("y", "z", "c", "x"))
    place = jnp.stack([y, z, c, x]).astype(jnp.int32)
    rolls, steps = queries.shape[:2]
    pair = NC * w_o.shape[1]
    width, hid = w_gate.shape
    cache = cache.transpose(0, 2, 1)
    hidden = hidden.transpose(1, 2, 0).reshape(-1, hidden.shape[0])
    w_o, w_gate, w_up = w_o.T, w_gate.T, w_up.T

    def other(v):
        return lax.ppermute(v, "c", shift(NC, 1))

    with jax.named_scope("attend"):
        depth = w_o.shape[1] // NY
        w_o = lax.all_to_all(cut(w_o, NY), "y", 0, 0)
        swapped = [other(v) for v in (hidden, w_gate, w_up, w_down)]
        head_out = attend(queries, new_entries, cache, lengths, w_uv)
        head_out, w_o, swapped = lax.optimization_barrier((head_out, w_o, swapped))
        hidden_alien, w_gate_alien, w_up_alien, w_down_alien = swapped

    with jax.named_scope("gather_heads"):
        w_o_alien = other(w_o)
        added = stream(place, hidden, hidden_alien, steps)
        near = lax.all_to_all(head_out.reshape(NY * NZ, -1, depth), ("y", "z"), 0, 0)
        near, w_o_alien, added = lax.optimization_barrier((near, w_o_alien, added))

    with jax.named_scope("project"):
        parts = project(place, near.reshape(-1, depth), (w_o, w_o_alien), added)

    with jax.named_scope("sum_heads"):
        parts = lax.all_to_all(parts, ("y", "x"), 0, 0)
        resid = sum_heads(parts)

    with jax.named_scope("gather_resid"):
        resid = lax.all_to_all(resid, "z", 0, 0)
        resid, ready = lax.optimization_barrier(
            (resid, (w_gate, w_up, w_gate_alien, w_up_alien))
        )
        blocks = fetch(resid, "y", NY)
        weights = stacked(ready)

    with jax.named_scope("gate_up"):
        gain = lax.dynamic_slice_in_dim(ffn_gain, x * width, width, 0).astype(F32)
        messages = gate_up(place, gain.reshape(NZ, pair), blocks, weights)

    with jax.named_scope("sum_gate_up"):
        messages = [messages[0]] + [
            lax.ppermute(messages[k], "x", shift(NX, k)) for k in range(1, NX)
        ]
        act = activate(messages, NX * width, hid)

    with jax.named_scope("down"):
        act, ready = lax.optimization_barrier((act, (w_down, w_down_alien)))
        act = fetch(act, "x", NX)
        out = down(place, act, stacked(ready))

    with jax.named_scope("sum_y"):
        out = lax.all_to_all(out.reshape(NY, -1, width), "y", 0, 0)
        out = sum_y(out)

    with jax.named_scope("sum_z"):
        out = lax.all_to_all(out.reshape(NZ, rolls * steps, width), "z", 0, 0)
        out = jnp.sum(out.astype(F32), axis=0)

    with jax.named_scope("finish"):
        at = (y * NZ + z) * steps
        own = jnp.stack([lax.dynamic_slice_in_dim(b, at, steps, 1) for b in blocks])
        own = jnp.concatenate([own, own], axis=0)
        own = lax.dynamic_slice_in_dim(own, lax.rem(NY - y, NY), NY, 0)
        own = own.transpose(0, 2, 1, 3).reshape(rolls * steps, width)
        out = (own.astype(F32) + out).astype(BF16)
    return out.reshape(rolls, steps, width)


def solution(mesh):
    fine = Mesh(mesh.devices.reshape(NY, NZ, NC, NX), ("y", "z", "c", "x"))
    dp = ("y", "z", "c")
    placed = (
        P(dp, None, "x", None),
        P(dp, None, None),
        P(dp, None, None),
        P(dp),
        P(None, None, dp),
        P("x", None, None),
        P("x", dp),
        P(),
        P("x", dp),
        P("x", dp),
        P(dp, "x"),
    )
    return jax.shard_map(
        on_device, mesh=fine, in_specs=placed, out_specs=P(dp, None, "x"), check_vma=False
    )
```
